32 devices in a mesh: fsdp: 4 (over z), ctx: 4 (over y, x), tp: 2 (over core).
Axes of the slice: x: 2, y: 2, z: 4, core: 2. Of those that a mesh axis runs over, the one named last changes fastest.
Arguments:
- hidden_in: bfloat16 [32768, 768], P(('fsdp', 'ctx')), may hold values from -6 to 6
- cotangent: bfloat16 [32768, 768], P(('fsdp', 'ctx')), may hold values from -6 to 6
- positions: int32 [32768], P(('fsdp', 'ctx')), may hold values from -1 to 8191, as said below
- norm_gain: bfloat16 [768], P(('fsdp', 'ctx')), may hold values from 0.5 to 1.5
- proj_z: bfloat16 [768, 1536], P(('fsdp', 'ctx'), 'tp'), may hold values from -0.21875 to 0.21875
- proj_x: bfloat16 [768, 1536], P(('fsdp', 'ctx'), 'tp'), may hold values from -0.21875 to 0.21875
- proj_bc: bfloat16 [768, 256], P(('fsdp', 'ctx')), may hold values from -0.21875 to 0.21875
- proj_dt: bfloat16 [768, 24], P(('fsdp', 'ctx'), 'tp'), may hold values from -0.21875 to 0.21875
- conv_inner: float32 [4, 1536], P(None, 'tp'), may hold values from -3 to 3
- conv_inner_bias: float32 [1536], P('tp'), may hold values from -0.5 to 0.5
- conv_state: float32 [4, 256], replicated, may hold values from -3 to 3
- conv_state_bias: float32 [256], replicated, may hold values from -0.5 to 0.5
- dt_bias: float32 [24], P('tp'), as said below
- a_log: float32 [24], P('tp'), may hold values from 0 to 2.77
- skip_gain: float32 [24], P('tp'), may hold values from 0.5 to 1.5
- gated_gain: float32 [1536], P('tp'), may hold values from 0.5 to 1.5
- proj_out: bfloat16 [1536, 768], P('tp', ('fsdp', 'ctx')), may hold values from -0.15625 to 0.15625
Outputs:
- hidden_out: bfloat16 [32768, 768], P(('fsdp', 'ctx'))
- grad_hidden: float32 [32768, 768], P(('fsdp', 'ctx'))
- grad_norm_gain: float32 [768], P(('fsdp', 'ctx'))
- grad_proj_z: float32 [768, 1536], P(('fsdp', 'ctx'), 'tp')
- grad_proj_x: float32 [768, 1536], P(('fsdp', 'ctx'), 'tp')
- grad_proj_bc: float32 [768, 256], P(('fsdp', 'ctx'))
- grad_proj_dt: float32 [768, 24], P(('fsdp', 'ctx'), 'tp')
- grad_conv_inner: float32 [4, 1536], P(None, 'tp')
- grad_conv_inner_bias: float32 [1536], P('tp')
- grad_conv_state: float32 [4, 256], replicated
- grad_conv_state_bias: float32 [256], replicated
- grad_dt_bias: float32 [24], P('tp')
- grad_a_log: float32 [24], P('tp')
- grad_skip_gain: float32 [24], P('tp')
- grad_gated_gain: float32 [1536], P('tp')
- grad_proj_out: float32 [1536, 768], P('tp', ('fsdp', 'ctx'))
The draws below stay inside these ranges and needn't reach their ends.
Inputs may be any that keep to these rules, and one draw needn't show every extreme that they name: `positions`: each group of 8192 consecutive rows (one index of fsdp) begins with a sequence at its first row and holds whole sequences of 2048 to 8192 rows one after another, each counted 0, 1, 2, ..., followed by its empty rows (-1), if any; groups hold different numbers of rows; some sequence has exactly 8192 rows. `dt_bias`: each entry is log(exp(dt) - 1) for a step dt between 0.01 / 8192 and 0.1.
All inputs are finite; a program needn't handle non-finite values.
Results may differ from the reference program's by a relative error of at most 0.0078.
Values may be sent and summed in bfloat16 or wider, within the bound.
A program may use at most 256 MiB of HBM per device.

```python
import math
import jax
import jax.numpy as jnp
from jax import lax

D = 768
INNER = 1536
HEAD_DIM = 64
STATE = 128
CONV = 4
BLOCK = 256
HEADS = 24
ROWS_GROUP = 8192
SEQ_MAX = 8192
SEQ_MIN = 2048
TOKENS = 32768


def draw_positions(key, part):
    groups = TOKENS // ROWS_GROUP
    slot_count = ROWS_GROUP // SEQ_MIN + 1
    key_len, key_cap = jax.random.split(jax.random.fold_in(key, 7))
    lengths = jax.random.randint(key_len, (groups, slot_count), SEQ_MIN, SEQ_MAX + 1)
    lengths = lengths.at[0, 0].set(SEQ_MAX)
    group_caps = jax.random.randint(key_cap, (groups,), ROWS_GROUP // 2, ROWS_GROUP + 1)
    group_caps = group_caps.at[0].set(ROWS_GROUP)
    lengths = lengths.at[:, 0].set(jnp.minimum(lengths[:, 0], group_caps))
    seq_ends = jnp.cumsum(lengths, axis=1)
    starts = seq_ends - lengths
    fitting = seq_ends <= group_caps[:, None]
    row_index = jnp.arange(ROWS_GROUP)
    inside = (row_index[None, None, :] >= starts[:, :, None]) & (row_index[None, None, :] < seq_ends[:, :, None]) & fitting[:, :, None]
    offsets = jnp.sum(jnp.where(inside, row_index[None, None, :] - starts[:, :, None], 0), axis=1)
    covered = jnp.any(inside, axis=1)
    return jnp.where(covered, offsets, -1).reshape(TOKENS).astype(jnp.int32)


def draw_dt_bias(key, part):
    unit = jax.random.uniform(jax.random.fold_in(key, 11), (HEADS,), jnp.float32)
    lower_log = math.log(0.01 / ROWS_GROUP)
    upper_log = math.log(0.1)
    step = jnp.exp(lower_log + unit * (upper_log - lower_log))
    return (step + jnp.log(-jnp.expm1(-step))).astype(jnp.float32)


def levels(key, extent, shards, low, largest):
    factor_of, own = 1.0, jax.random.fold_in(key, 6)
    for axis_at, shards_of in shards:
        steps = jnp.exp(jax.random.uniform(jax.random.fold_in(own, axis_at), (shards_of,), jnp.float32, low / len(shards), largest / len(shards)))
        factor_of = factor_of * jnp.repeat(steps, extent[axis_at] // shards_of).reshape([-1 if axis == axis_at else 1 for axis in range(len(extent))])
    return factor_of


def normal_values(stream_key, dims, scale, bound, shards=(), kind=jnp.bfloat16):
    loudness = levels(stream_key, dims, shards, -0.22, 0.18) if shards else 1.0
    drawn = jax.random.normal(stream_key, dims, jnp.float32) * scale * loudness
    return jnp.minimum(jnp.maximum(drawn, -bound), bound).astype(kind)


def setup_inputs(seed: int = 0) -> dict:
    key_list = jax.random.split(jax.random.key(seed), 18)
    return {
        "hidden_in": normal_values(key_list[0], (TOKENS, D), 1.0, 6.0, ((0, 16),)),
        "cotangent": normal_values(key_list[1], (TOKENS, D), 1.0, 6.0, ((0, 16),)),
        "positions": draw_positions(jax.random.fold_in(key_list[17], 71), 0),
        "norm_gain": jnp.clip(1.0 + 0.1 * jax.random.normal(key_list[3], (D,), jnp.float32), 0.5, 1.5).astype(jnp.bfloat16),
        "proj_z": normal_values(key_list[4], (D, INNER), D ** -0.5, 0.21875, ((0, 16), (1, 2))),
        "proj_x": normal_values(key_list[5], (D, INNER), D ** -0.5, 0.21875, ((0, 16), (1, 2))),
        "proj_bc": normal_values(key_list[6], (D, 2 * STATE), D ** -0.5, 0.21875, ((0, 16),)),
        "proj_dt": normal_values(key_list[7], (D, HEADS), D ** -0.5, 0.21875, ((0, 16), (1, 2))),
        "conv_inner": normal_values(key_list[8], (CONV, INNER), CONV ** -0.5, 3.0, ((1, 2),), jnp.float32),
        "conv_inner_bias": jnp.clip(jax.random.uniform(key_list[9], (INNER,), jnp.float32, -0.5, 0.5) * levels(key_list[9], (INNER,), ((0, 2),), -0.4, 0.0), -0.5, 0.5),
        "conv_state": normal_values(key_list[10], (CONV, 2 * STATE), CONV ** -0.5, 3.0, (), jnp.float32),
        "conv_state_bias": jnp.clip(jax.random.uniform(key_list[11], (2 * STATE,), jnp.float32, -0.5, 0.5), -0.5, 0.5),
        "dt_bias": draw_dt_bias(jax.random.fold_in(key_list[17], 71), 0),
        "a_log": jnp.clip(2.77 * jax.random.uniform(key_list[13], (HEADS,), jnp.float32) ** levels(key_list[13], (HEADS,), ((0, 2),), -0.2, 0.2), 0.0, 2.77),
        "skip_gain": jnp.clip(0.5 + 1.0 * jax.random.uniform(key_list[14], (HEADS,), jnp.float32) ** levels(key_list[14], (HEADS,), ((0, 2),), -0.2, 0.2), 0.5, 1.5),
        "gated_gain": jnp.clip(1.0 + 0.1 * jax.random.normal(key_list[15], (INNER,), jnp.float32), 0.5, 1.5),
        "proj_out": normal_values(key_list[16], (INNER, D), INNER ** -0.5, 0.15625, ((0, 2), (1, 16))),
    }


EPS = 1e-05
HIGHEST = lax.Precision.HIGHEST

@jax.custom_vjp
def low(v):
    return lax.optimization_barrier(v.astype(jnp.bfloat16)).astype(jnp.float32)

@jax.custom_vjp
def low_back(v):
    return v

def low_keep(v):
    return (low(v), None)

def low_pass(kept, grad):
    return (grad,)

def back_keep(v):
    return (v, None)

def back_low(kept, grad):
    return (low(grad),)
low.defvjp(low_keep, low_pass)
low_back.defvjp(back_keep, back_low)

def product(left, right):
    return jnp.dot(left, right, precision=HIGHEST)

def causal_conv(extended, weight, biases, positions):
    row_count = positions.shape[0]
    tap_count = weight.shape[0]
    totals = jnp.broadcast_to(biases[None, :], (row_count, biases.shape[0]))
    for offset in range(tap_count):
        window = lax.slice_in_dim(extended, tap_count - 1 - offset, tap_count - 1 - offset + row_count, axis=0)
        masked = (positions >= offset).astype(jnp.float32)[:, None]
        totals = totals + weight[offset][None, :] * window * masked
    return totals

def block_step(carry_state, inputs):
    decay_log, inner_u, state_b, state_c, starts = inputs
    block_rows = starts.shape[0]
    cumulative = jnp.cumsum(decay_log, axis=0)
    segment = jnp.cumsum(starts)
    row_index = jnp.arange(block_rows)
    same_seq = jnp.logical_and(row_index[:, None] >= row_index[None, :], segment[:, None] == segment[None, :])[:, :, None]
    spread = cumulative[:, None, :] - cumulative[None, :, :]
    within = jnp.where(same_seq, jnp.exp(jnp.where(same_seq, spread, 0.0)), 0.0)
    scores = jnp.dot(state_c, state_b.T, precision=HIGHEST)
    intra_out = jnp.einsum('ijh,jhp->ihp', within * scores[:, :, None], inner_u, precision=HIGHEST)
    entry_decay = jnp.exp(cumulative) * (segment == 0).astype(jnp.float32)[:, None]
    carried = jnp.einsum('hpn,in->ihp', carry_state, state_c, precision=HIGHEST) * entry_decay[:, :, None]
    closing = (segment == segment[-1])[:, None]
    towards = jnp.where(closing, jnp.exp(cumulative[-1][None, :] - cumulative), 0.0)
    through = jnp.exp(cumulative[-1]) * (segment[-1] == 0).astype(jnp.float32)
    fresh_state = jnp.einsum('jh,jhp,jn->hpn', towards, inner_u, state_b, precision=HIGHEST)
    return (through[:, None, None] * carry_state + fresh_state, intra_out + carried)

def group_scan(group_items):
    start_state = jnp.zeros((HEADS, HEAD_DIM, STATE), jnp.float32)
    final_state, group_out = lax.scan(jax.checkpoint(block_step), start_state, group_items)
    return group_out

def forward_block(positions, hidden, norm_gain, proj_z, proj_x, proj_bc, proj_dt, conv_inner, conv_inner_bias, conv_state, conv_state_bias, dt_bias, a_log, skip_gain, gated_gain, proj_out):
    row_count = hidden.shape[0]
    row_scale = lax.rsqrt(lax.optimization_barrier(jnp.mean(hidden * hidden, axis=1, keepdims=True)) + EPS)
    normed = low(hidden * row_scale * norm_gain[None, :])
    gate_z = low_back(product(normed, proj_z))
    inner_x = low_back(product(normed, proj_x))
    state_in = low_back(product(normed, proj_bc))
    step_raw = low_back(product(normed, proj_dt))
    rim_rows = conv_inner.shape[0] - 1
    pad_x = jnp.concatenate([jnp.zeros((rim_rows, inner_x.shape[1]), jnp.float32), inner_x], axis=0)
    pad_bc = jnp.concatenate([jnp.zeros((rim_rows, state_in.shape[1]), jnp.float32), state_in], axis=0)
    conv_x = jax.nn.silu(causal_conv(pad_x, conv_inner, conv_inner_bias, positions))
    conv_bc = jax.nn.silu(causal_conv(pad_bc, conv_state, conv_state_bias, positions))
    state_b = conv_bc[:, :STATE]
    state_c = conv_bc[:, STATE:]
    step_size = jax.nn.softplus(step_raw + dt_bias[None, :])
    decay_rate = -jnp.exp(a_log)
    decay_log = step_size * decay_rate[None, :]
    heads_x = conv_x.reshape(row_count, HEADS, HEAD_DIM)
    inner_u = heads_x * step_size[:, :, None]
    starts = (positions == 0).astype(jnp.float32)
    group_count = row_count // ROWS_GROUP
    blocks = ROWS_GROUP // BLOCK
    scanned = lax.map(group_scan, (decay_log.reshape(group_count, blocks, BLOCK, HEADS), inner_u.reshape(group_count, blocks, BLOCK, HEADS, HEAD_DIM), state_b.reshape(group_count, blocks, BLOCK, STATE), state_c.reshape(group_count, blocks, BLOCK, STATE), starts.reshape(group_count, blocks, BLOCK)))
    mixed_out = scanned.reshape(row_count, HEADS, HEAD_DIM) + skip_gain[None, :, None] * heads_x
    gated_out = mixed_out.reshape(row_count, INNER) * jax.nn.silu(gate_z)
    gated_scale = lax.rsqrt(lax.optimization_barrier(jnp.mean(gated_out * gated_out, axis=1, keepdims=True)) + EPS)
    gnormed = low(gated_out * gated_scale * gated_gain[None, :])
    branch = product(gnormed, proj_out)
    row_valid = (positions >= 0).astype(jnp.float32)
    return hidden + branch * row_valid[:, None]

def reference(hidden_in, cotangent, positions, norm_gain, proj_z, proj_x, proj_bc, proj_dt, conv_inner, conv_inner_bias, conv_state, conv_state_bias, dt_bias, a_log, skip_gain, gated_gain, proj_out):
    floats = tuple((argument.astype(jnp.float32) for argument in (hidden_in, norm_gain, proj_z, proj_x, proj_bc, proj_dt, conv_inner, conv_inner_bias, conv_state, conv_state_bias, dt_bias, a_log, skip_gain, gated_gain, proj_out)))

    def closed(*arrays):
        return forward_block(positions, *arrays)
    output, pullback = jax.vjp(closed, *floats)
    gradients = pullback(cotangent.astype(jnp.float32))
    return (output.astype(jnp.bfloat16), gradients[0], gradients[1], gradients[2], gradients[3], gradients[4], gradients[5], gradients[6], gradients[7], gradients[8], gradients[9], gradients[10], gradients[11], gradients[12], gradients[13], gradients[14])
```

```python
import functools

import jax
import jax.numpy as jnp
from jax import lax
from jax.experimental import pallas as pl
from jax.experimental.pallas import tpu as pltpu
from jax.sharding import PartitionSpec as P

INNER = 1536
BLOCK = 256


EPS = 1e-05
HIGHEST = lax.Precision.HIGHEST


def passed_along(value, axis, steps):
    count = lax.axis_size(axis)
    initial, last = (max(0, -steps), min(count, count - steps))
    return lax.ppermute(value, axis, [(source, source + steps) for source in range(initial, last)])


def pair_sum(value, axis):
    if lax.axis_size(axis) != 2:
        return lax.psum(value, axis)
    return value + lax.ppermute(value, axis, [(0, 1), (1, 0)])


def entering(decay, state, axis, backward):
    count, mine = (lax.axis_size(axis), lax.axis_index(axis))
    decays, states = (lax.all_gather(decay, axis), lax.all_gather(state, axis))
    running = jnp.zeros_like(state)
    for step in range(count - 1):
        at = count - 1 - step if backward else step
        joined = decays[at] * running + states[at]
        running = jnp.where(at > mine if backward else at < mine, joined, running)
    return running


def silu_grad(values):
    logistic = jax.nn.sigmoid(values)
    return logistic * (1.0 + values * (1.0 - logistic))


def contract_last(left, right):
    return lax.dot_general(
        left, right, (((1,), (1,)), ((), ())), preferred_element_type=jnp.float32
    )


def contract_rows(left, right):
    return lax.dot_general(
        left, right, (((0,), (0,)), ((), ())), preferred_element_type=jnp.float32
    )


def causal_conv(extended, weight, biases, positions):
    row_count = positions.shape[0]
    tap_count = weight.shape[0]
    totals = jnp.broadcast_to(biases[None, :], (row_count, biases.shape[0]))
    for offset in range(tap_count):
        window = lax.slice_in_dim(
            extended, tap_count - 1 - offset, tap_count - 1 - offset + row_count, axis=0
        )
        masked = (positions >= offset).astype(jnp.float32)[:, None]
        totals = totals + weight[offset][None, :] * window * masked
    return totals


def conv_back(grads_pre, extended, weight, positions):
    row_count = positions.shape[0]
    tap_count = weight.shape[0]
    spread = None
    weight_grads = []
    for offset in range(tap_count):
        masked = grads_pre * (positions >= offset).astype(jnp.float32)[:, None]
        window = lax.slice_in_dim(
            extended, tap_count - 1 - offset, tap_count - 1 - offset + row_count, axis=0
        )
        weight_grads.append(jnp.sum(masked * window, axis=0))
        term = jnp.pad(
            weight[offset][None, :] * masked, ((tap_count - 1 - offset, offset), (0, 0))
        )
        spread = term if spread is None else spread + term
    return (jnp.stack(weight_grads), jnp.sum(grads_pre, axis=0), spread)


NN = (((1,), (0,)), ((), ()))
NT = (((1,), (1,)), ((), ()))
TN = (((0,), (0,)), ((), ()))


def dot_full(left, right, dims):
    return lax.dot_general(
        left, right, dims, precision=HIGHEST, preferred_element_type=jnp.float32
    )


def first_half(rows, width):
    return lax.broadcasted_iota(jnp.int32, (rows, 2 * width), 1) < width


def spread_pair(factors, pair, first):
    return jnp.where(
        first, factors[:, 2 * pair : 2 * pair + 1], factors[:, 2 * pair + 1 : 2 * pair + 2]
    )


def state_kernel(width, factor_ref, left_ref, right_ref, out_ref):
    rows = left_ref.shape[0]
    first = first_half(rows, width)
    factors, right = (factor_ref[...], right_ref[...])
    for pair in range(factor_ref.shape[1] // 2):
        columns = slice(2 * width * pair, 2 * width * (pair + 1))
        scaled = left_ref[:, columns] * spread_pair(factors, pair, first)
        out_ref[columns, :] = dot_full(scaled, right, TN)


def allowed_bias(seg_col, seg_row):
    rows = seg_col.shape[0]
    later = lax.broadcasted_iota(jnp.int32, (rows, rows), 0)
    earlier = lax.broadcasted_iota(jnp.int32, (rows, rows), 1)
    allowed = jnp.logical_and(later >= earlier, seg_col == seg_row)
    return jnp.where(allowed, 0.0, -1e30)


def scan_kernel(
    width, cum_ref, cum_t_ref, seg_ref, seg_t_ref, entry_ref, u_ref, b_ref, c_ref, in_ref, out_ref
):
    rows = u_ref.shape[0]
    first = first_half(rows, width)
    state_c = c_ref[...]
    scores = dot_full(state_c, b_ref[...], NT)
    bias = allowed_bias(seg_ref[...], seg_t_ref[...])
    entry = entry_ref[...]
    for pair in range(entry_ref.shape[1] // 2):
        columns = slice(2 * width * pair, 2 * width * (pair + 1))
        inner_u = u_ref[:, columns]
        carried = dot_full(state_c, in_ref[columns, :], NT) * spread_pair(entry, pair, first)
        parts = []
        for head in (2 * pair, 2 * pair + 1):
            gap = cum_ref[:, head : head + 1] - cum_t_ref[head : head + 1, :]
            parts.append(dot_full(jnp.exp(gap + bias) * scores, inner_u, NN))
        out_ref[:, columns] = carried + jnp.where(first, parts[0], parts[1])


def back_kernel(
    width,
    cum_ref,
    cum_t_ref,
    seg_ref,
    seg_t_ref,
    entry_ref,
    towards_ref,
    u_ref,
    dy_ref,
    b_ref,
    c_ref,
    in_ref,
    out_grad_ref,
    grad_u_ref,
    grad_cum_ref,
    grad_cum_t_ref,
    grad_b_ref,
    grad_c_ref,
):
    rows = u_ref.shape[0]
    first = first_half(rows, width)
    state_b, state_c = (b_ref[...], c_ref[...])
    scores = dot_full(state_c, state_b, NT)
    bias = allowed_bias(seg_ref[...], seg_t_ref[...])
    entry, towards = (entry_ref[...], towards_ref[...])
    last_row = lax.broadcasted_iota(jnp.int32, (rows, 1), 0) == rows - 1
    grad_scores = jnp.zeros((rows, rows), jnp.float32)
    grad_b = jnp.zeros(state_b.shape, jnp.float32)
    grad_c = jnp.zeros(state_c.shape, jnp.float32)
    for pair in range(entry_ref.shape[1] // 2):
        columns = slice(2 * width * pair, 2 * width * (pair + 1))
        inner_u, grad_y = (u_ref[:, columns], dy_ref[:, columns])
        state_in, grad_out = (in_ref[columns, :], out_grad_ref[columns, :])
        entry_pair = spread_pair(entry, pair, first)
        towards_pair = spread_pair(towards, pair, first)
        from_later = dot_full(state_b, grad_out, NT)
        from_earlier = dot_full(state_c, state_in, NT)
        grad_c = grad_c + dot_full(entry_pair * grad_y, state_in, NN)
        grad_b = grad_b + dot_full(towards_pair * inner_u, grad_out, NN)
        later_dot = from_later * inner_u * towards_pair
        earlier_dot = from_earlier * grad_y * entry_pair
        parts = []
        for half in (0, 1):
            head = 2 * pair + half
            mine = first if half == 0 else jnp.logical_not(first)
            gap = cum_ref[:, head : head + 1] - cum_t_ref[head : head + 1, :]
            within = jnp.exp(gap + bias)
            parts.append(dot_full(within * scores, grad_y, TN))
            grad_mix = dot_full(jnp.where(mine, grad_y, 0.0), inner_u, NT) * within
            grad_scores = grad_scores + grad_mix
            pulled = grad_mix * scores
            moved = jnp.sum(jnp.where(mine, later_dot, 0.0), axis=1, keepdims=True)
            entered = jnp.sum(jnp.where(mine, earlier_dot, 0.0), axis=1, keepdims=True)
            total = jnp.sum(moved, axis=0, keepdims=True)
            grad_cum_ref[:, head : head + 1] = (
                jnp.sum(pulled, axis=1, keepdims=True)
                + entered
                - moved
                + jnp.where(last_row, total, 0.0)
            )
            grad_cum_t_ref[head : head + 1, :] = jnp.sum(pulled, axis=0, keepdims=True)
        grad_u_ref[:, columns] = (
            jnp.where(first, parts[0], parts[1]) + towards_pair * from_later
        )
    grad_b_ref[...] = grad_b + dot_full(grad_scores, state_c, TN)
    grad_c_ref[...] = grad_c + dot_full(grad_scores, state_b, NN)


def by_blocks(kernel, operands, outs, block_count):
    def spec(shape):
        return pl.BlockSpec((None, *shape[1:]), lambda at: (at,) + (0,) * (len(shape) - 1))

    return pl.pallas_call(
        kernel,
        grid=(block_count,),
        in_specs=[spec(operand.shape) for operand in operands],
        out_specs=[spec(shape) for shape in outs],
        out_shape=[jax.ShapeDtypeStruct(shape, jnp.float32) for shape in outs],
        compiler_params=pltpu.CompilerParams(vmem_limit_bytes=48 * 1024 * 1024),
    )(*operands)


def chained(through, local, reverse):
    order = range(local.shape[0])
    factor, running = (jnp.ones_like(through[0]), jnp.zeros_like(local[0]))
    factors, states = ([], [])
    for at in reversed(order) if reverse else order:
        factors.append(factor)
        states.append(running)
        factor, running = (factor * through[at], through[at] * running + local[at])
    if reverse:
        factors, states = (factors[::-1], states[::-1])
    return (factor, running, jnp.stack(factors), jnp.stack(states))


def summed_rows(value, groups):
    return lax.psum_scatter(value, groups, scatter_dimension=0, tiled=True)


def on_device(
    hidden_in,
    cotangent,
    positions,
    norm_gain,
    proj_z,
    proj_x,
    proj_bc,
    proj_dt,
    conv_inner,
    conv_inner_bias,
    conv_state,
    conv_state_bias,
    dt_bias,
    a_log,
    skip_gain,
    gated_gain,
    proj_out,
):
    row_count = hidden_in.shape[0]
    full_width = hidden_in.shape[1]
    tap_count = conv_inner.shape[0]
    rim_rows = tap_count - 1
    local_inner = proj_z.shape[1]
    local_heads = proj_dt.shape[1]
    head_width = local_inner // local_heads
    state_width = proj_bc.shape[1] // 2
    block_count = row_count // BLOCK
    groups = ("fsdp", "ctx")
    spare = jnp.zeros((proj_dt.shape[0], 128 - local_heads - 1), jnp.bfloat16)
    early = jnp.concatenate([proj_x, proj_bc, proj_dt, norm_gain[:, None], spare], axis=1)
    early = lax.all_gather(early, groups, axis=0, tiled=True)
    late = jnp.concatenate([proj_z, proj_out.T], axis=1)
    late = lax.all_gather(late, groups, axis=0, tiled=True)
    bc_end = local_inner + 2 * state_width
    weight_x, weight_bc = (early[:, :local_inner], early[:, local_inner:bc_end])
    weight_dt = early[:, bc_end : bc_end + local_heads]
    gain_full = early[:, bc_end + local_heads]
    weight_z, weight_out_t = (late[:, :local_inner], late[:, local_inner:])
    row_valid = (positions >= 0).astype(jnp.float32)
    starts = (positions == 0).astype(jnp.float32)
    hidden = hidden_in.astype(jnp.float32)
    row_scale = lax.rsqrt(jnp.mean(hidden * hidden, axis=1, keepdims=True) + EPS)
    normed = (hidden * row_scale * gain_full.astype(jnp.float32)[None, :]).astype(jnp.bfloat16)
    gate_z = jnp.dot(normed, weight_z, preferred_element_type=jnp.float32)
    inner_x = jnp.dot(normed, weight_x, preferred_element_type=jnp.float32)
    state_in = jnp.dot(normed, weight_bc, preferred_element_type=jnp.float32)
    step_raw = jnp.dot(normed, weight_dt, preferred_element_type=jnp.float32)
    rim_x, rim_bc = passed_along(
        (inner_x[row_count - rim_rows :], state_in[row_count - rim_rows :]), "ctx", 1
    )
    ext_x = jnp.concatenate([rim_x, inner_x], axis=0)
    ext_bc = jnp.concatenate([rim_bc, state_in], axis=0)
    pre_x = causal_conv(ext_x, conv_inner, conv_inner_bias, positions)
    pre_bc = causal_conv(ext_bc, conv_state, conv_state_bias, positions)
    conv_x = jax.nn.silu(pre_x)
    conv_bc = jax.nn.silu(pre_bc)
    state_b = conv_bc[:, :state_width]
    state_c = conv_bc[:, state_width:]
    shifted_step = step_raw + dt_bias[None, :]
    step_size = jax.nn.softplus(shifted_step)
    decay_rate = -jnp.exp(a_log)
    decay_log = step_size * decay_rate[None, :]
    inner_u = conv_x * jnp.repeat(step_size, head_width, axis=1)
    decay_blocks = decay_log.reshape(block_count, BLOCK, local_heads)
    start_blocks = starts.reshape(block_count, BLOCK)
    row_index = jnp.arange(BLOCK)
    lower = (row_index[:, None] >= row_index[None, :]).astype(jnp.float32)
    cumulative = jnp.einsum("ij,cjh->cih", lower, decay_blocks, precision=HIGHEST)
    segment = jnp.einsum("ij,cj->ci", lower, start_blocks, precision=HIGHEST)
    entry_decay = jnp.exp(cumulative) * (segment == 0).astype(jnp.float32)[:, :, None]
    closing = (segment == segment[:, -1:])[:, :, None]
    towards = jnp.where(closing, jnp.exp(cumulative[:, -1:] - cumulative), 0.0)
    through = entry_decay[:, -1]
    through_rows = jnp.repeat(through, head_width, axis=1)[:, :, None]
    cumulative_t = cumulative.transpose(0, 2, 1)
    seg_col, seg_row = (segment[:, :, None], segment[:, None, :])
    u_blocks = inner_u.reshape(block_count, BLOCK, local_inner)
    b_blocks = state_b.reshape(block_count, BLOCK, state_width)
    c_blocks = state_c.reshape(block_count, BLOCK, state_width)
    rows_shape = (block_count, BLOCK, local_inner)
    state_shape = (block_count, local_inner, state_width)
    side_shape = (block_count, BLOCK, state_width)
    make_state = functools.partial(state_kernel, head_width)
    (local_state,) = by_blocks(make_state, (towards, u_blocks, b_blocks), [state_shape], block_count)
    piece_decay, piece_state, prefix_decay, prefix_state = chained(
        through_rows, local_state, False
    )
    incoming = entering(piece_decay, piece_state, "ctx", False)
    block_in = prefix_decay * incoming[None] + prefix_state
    (scanned,) = by_blocks(
        functools.partial(scan_kernel, head_width),
        (
            cumulative,
            cumulative_t,
            seg_col,
            seg_row,
            entry_decay,
            u_blocks,
            b_blocks,
            c_blocks,
            block_in,
        ),
        [rows_shape],
        block_count,
    )
    skip_row = jnp.repeat(skip_gain, head_width)[None, :]
    mixed_out = scanned.reshape(row_count, local_inner) + skip_row * conv_x
    gate_act = jax.nn.silu(gate_z)
    gated_out = mixed_out * gate_act
    squares = pair_sum(jnp.sum(gated_out * gated_out, axis=1), "tp")
    gated_scale = lax.rsqrt(squares / INNER + EPS)[:, None]
    gnormed = (gated_out * gated_scale * gated_gain[None, :]).astype(jnp.bfloat16)
    partial_branch = contract_last(gnormed, weight_out_t)
    branch = pair_sum(partial_branch, "tp")
    hidden_out = (hidden + branch * row_valid[:, None]).astype(jnp.bfloat16)
    grad_branch = (cotangent.astype(jnp.float32) * row_valid[:, None]).astype(jnp.bfloat16)
    grad_wout_t = contract_rows(grad_branch, gnormed)
    grad_gnormed = jnp.dot(grad_branch, weight_out_t, preferred_element_type=jnp.float32)
    weighted = grad_gnormed * gated_gain[None, :]
    grad_ggain = jnp.sum(grad_gnormed * gated_out * gated_scale, axis=0)
    gated_dot = pair_sum(jnp.sum(weighted * gated_out, axis=1), "tp")[:, None]
    grad_gated = gated_scale * weighted - gated_out * gated_scale**3 * gated_dot / INNER
    grad_mixed = grad_gated * gate_act
    grad_z = (grad_gated * mixed_out * silu_grad(gate_z)).astype(jnp.bfloat16)
    grad_wz = contract_rows(normed, grad_z)
    grads_early = summed_rows(jnp.concatenate([grad_wout_t, grad_wz], axis=1), groups)
    grad_skip = jnp.sum((grad_mixed * conv_x).sum(axis=0).reshape(local_heads, head_width), axis=1)
    grad_y_blocks = grad_mixed.reshape(block_count, BLOCK, local_inner)
    (local_back,) = by_blocks(
        make_state, (entry_decay, grad_y_blocks, c_blocks), [state_shape], block_count
    )
    piece_factor, piece_back, suffix_decay, suffix_back = chained(through_rows, local_back, True)
    outgoing = entering(piece_decay, piece_back, "ctx", True)
    grad_out_blocks = suffix_decay * outgoing[None] + suffix_back
    head_rows = (block_count, BLOCK, local_heads)
    grad_u, grad_cum, grad_cum_t, grad_b, grad_c = by_blocks(
        functools.partial(back_kernel, head_width),
        (
            cumulative,
            cumulative_t,
            seg_col,
            seg_row,
            entry_decay,
            towards,
            u_blocks,
            grad_y_blocks,
            b_blocks,
            c_blocks,
            block_in,
            grad_out_blocks,
        ),
        [rows_shape, head_rows, (block_count, local_heads, BLOCK), side_shape, side_shape],
        block_count,
    )
    passed = (grad_out_blocks * block_in).reshape(block_count, local_heads, -1).sum(axis=2)
    grad_cum = grad_cum - grad_cum_t.transpose(0, 2, 1)
    grad_decay = jnp.einsum("ji,cjh->cih", lower, grad_cum, precision=HIGHEST)
    grad_decay = (grad_decay + (passed * through)[:, None, :]).reshape(row_count, local_heads)
    grad_u = grad_u.reshape(row_count, local_inner)
    step_rows = jnp.repeat(step_size, head_width, axis=1)
    grad_step = grad_decay * decay_rate[None, :] + jnp.sum(
        (grad_u * conv_x).reshape(row_count, local_heads, head_width), axis=2
    )
    grad_alog = jnp.sum(grad_decay * step_size, axis=0) * decay_rate
    grad_shift = grad_step * jax.nn.sigmoid(shifted_step)
    grad_dtbias = jnp.sum(grad_shift, axis=0)
    grad_raw = grad_shift.astype(jnp.bfloat16)
    grad_heads = grad_u * step_rows + skip_row * grad_mixed
    grad_pre_x = grad_heads * silu_grad(pre_x)
    grad_bc_part = jnp.concatenate(
        [grad_b.reshape(row_count, state_width), grad_c.reshape(row_count, state_width)], axis=1
    )
    grad_conv_bc = pair_sum(grad_bc_part, "tp")
    grad_pre_bc = grad_conv_bc * silu_grad(pre_bc)
    wgrad_x, bgrad_x, spread_x = conv_back(grad_pre_x, ext_x, conv_inner, positions)
    wgrad_bc, bgrad_bc, spread_bc = conv_back(grad_pre_bc, ext_bc, conv_state, positions)
    later_x, later_bc = passed_along((spread_x[:rim_rows], spread_bc[:rim_rows]), "ctx", -1)
    grad_inner_x = spread_x[rim_rows:].at[row_count - rim_rows :].add(later_x).astype(jnp.bfloat16)
    grad_state_in = (
        spread_bc[rim_rows:].at[row_count - rim_rows :].add(later_bc).astype(jnp.bfloat16)
    )
    first_tp = (lax.axis_index("tp") == 0).astype(jnp.float32)
    partial_grad = (
        contract_last(grad_z, weight_z)
        + contract_last(grad_inner_x, weight_x)
        + contract_last(grad_raw, weight_dt)
        + first_tp * contract_last(grad_state_in, weight_bc)
    )
    grad_normed = pair_sum(partial_grad, "tp")
    pulled = grad_normed * gain_full.astype(jnp.float32)[None, :]
    norm_dot = jnp.sum(pulled * hidden, axis=1, keepdims=True)
    grad_hidden = (
        row_scale * pulled
        - hidden * row_scale**3 * norm_dot / full_width
        + cotangent.astype(jnp.float32)
    )
    grad_gain = jnp.sum(grad_normed * hidden * row_scale, axis=0)
    grad_wx = contract_rows(normed, grad_inner_x)
    grad_wbc = contract_rows(normed, grad_state_in)
    grad_wdt = contract_rows(normed, grad_raw)
    filler = jnp.zeros((full_width, 128 - local_heads - 1), jnp.float32)
    grads_late = summed_rows(
        jnp.concatenate([grad_wx, grad_wbc, grad_wdt, grad_gain[:, None], filler], axis=1), groups
    )
    scattered = (
        grads_late[:, bc_end + local_heads],
        grads_early[:, local_inner:],
        grads_late[:, :local_inner],
        grads_late[:, local_inner:bc_end],
        grads_late[:, bc_end : bc_end + local_heads],
        grads_early[:, :local_inner].T,
    )
    small = (grad_ggain, wgrad_x, bgrad_x, wgrad_bc, bgrad_bc, grad_dtbias, grad_alog, grad_skip)
    flat = lax.psum(jnp.concatenate([part.reshape(-1) for part in small]), groups)
    reduced_small = []
    for part in small:
        reduced_small.append(flat[: part.size].reshape(part.shape))
        flat = flat[part.size :]
    return (
        hidden_out,
        grad_hidden,
        scattered[0],
        scattered[1],
        scattered[2],
        scattered[3],
        scattered[4],
        reduced_small[1],
        reduced_small[2],
        reduced_small[3],
        reduced_small[4],
        reduced_small[5],
        reduced_small[6],
        reduced_small[7],
        reduced_small[0],
        scattered[5],
    )


def solution(mesh):
    placed = (
        P(("fsdp", "ctx"), None),
        P(("fsdp", "ctx"), None),
        P(("fsdp", "ctx")),
        P(("fsdp", "ctx")),
        P(("fsdp", "ctx"), "tp"),
        P(("fsdp", "ctx"), "tp"),
        P(("fsdp", "ctx"), None),
        P(("fsdp", "ctx"), "tp"),
        P(None, "tp"),
        P("tp"),
        P(),
        P(),
        P("tp"),
        P("tp"),
        P("tp"),
        P("tp"),
        P("tp", ("fsdp", "ctx")),
    )
    return jax.shard_map(
        on_device,
        mesh=mesh,
        in_specs=placed,
        out_specs=(
            P(("fsdp", "ctx"), None),
            P(("fsdp", "ctx"), None),
            P(("fsdp", "ctx")),
            P(("fsdp", "ctx"), "tp"),
            P(("fsdp", "ctx"), "tp"),
            P(("fsdp", "ctx"), None),
            P(("fsdp", "ctx"), "tp"),
            P(None, "tp"),
            P("tp"),
            P(),
            P(),
            P("tp"),
            P("tp"),
            P("tp"),
            P("tp"),
            P("tp", ("fsdp", "ctx")),
        ),
        check_vma=False,
    )
```
